32 devices in a mesh: section: 1, expert: 32 (over z, y, x, core).
Axes of the slice: x: 2, y: 2, z: 4, core: 2. Of those that a mesh axis runs over, the one named last changes fastest.
Arguments:
- act_send: bfloat16 [256, 3584], P(('section', 'expert')), may hold values from -6 to 6
- grad_send: bfloat16 [256, 3584], P(('section', 'expert')), may hold values from -6 to 6
- x_back: bfloat16 [256, 3584], P(('section', 'expert')), may hold values from -6 to 6
- routes_fwd: int32 [256, 2], P(('section', 'expert')), may hold values from 0 to 3, all different within a row; in each aligned block of 8 rows (0 to 7, 8 to 15, ...) at most 8 rows name the same one
- gates_fwd: float32 [256, 2], P(('section', 'expert')), may hold values from 0.3 to 1
- routes_back: int32 [256, 2], P(('section', 'expert')), may hold values from 0 to 3, all different within a row; in each aligned block of 8 rows (0 to 7, 8 to 15, ...) at most 8 rows name the same one
- gates_back: float32 [256, 2], P(('section', 'expert')), may hold values from 0.3 to 1
- norm_gain: float32 [1, 3584], P('section'), may hold values from 0.5 to 1.5
- w_gate: bfloat16 [1, 32, 3584, 128], P('section', 'expert'), may hold values from -0.09375 to 0.09375
- w_up: bfloat16 [1, 32, 3584, 128], P('section', 'expert'), may hold values from -0.09375 to 0.09375
- w_down: bfloat16 [1, 32, 128, 3584], P('section', 'expert'), may hold values from -0.1875 to 0.1875
- stash: bfloat16 [1, 32, 32, 8, 256], P('section', 'expert'), may hold values from -6 to 6
Outputs:
- outbound: bfloat16 [256, 3584], P(('section', 'expert'))
- input_grad: bfloat16 [256, 3584], P(('section', 'expert'))
The draws below stay inside these ranges and needn't reach their ends.
Inputs may be any that keep to these rules, and one draw needn't show every extreme that they name: `routes_fwd`: each row names 2 different experts; among the rows of one device no expert is named more than 8 times, a bound that some block reaches. `routes_back`: each row names 2 different experts; among the rows of one device no expert is named more than 8 times, a bound that some block reaches.
All inputs are finite; a program needn't handle non-finite values.
Results may differ from the reference program's by a relative error of at most 0.0055.
Values may be sent and summed in bfloat16 or wider, within the bound.
No kernel may reach another device: no remote copies, remote signals or barrier semaphores. Data moves between devices by JAX's collectives and lax.ppermute only.
A program may use at most 64 MiB of HBM per device.

```python
import math
import jax
import jax.numpy as jnp
import numpy as np
from jax import lax

D = 3584
HID_DEV = 128
TOP = 2
TOK_DEV = 8
SPLIT = 8
EXP_HIDDEN = 1024
EXPERTS = 4
CAP = 8
TOKENS = 256
N_SECTION = 1
N_EXPERT = 32


def levels(own_key, extent, pieces, least, top_value):
    factor_of = 1.0
    for axis_at, shards_of in pieces:
        steps = jax.random.uniform(jax.random.fold_in(jax.random.fold_in(own_key, 6), axis_at), (shards_of,), jnp.float32, least / len(pieces), top_value / len(pieces))
        factor_of = factor_of * jnp.repeat(jnp.exp(steps), extent[axis_at] // shards_of).reshape((-1,) + (1,) * (len(extent) - 1 - axis_at))
    return factor_of


def assign_block(own_key, own, number, rows, amount, top, most, lean):
    order = jax.random.permutation(own_key, amount)
    packed, ordinary = load_shares(amount, rows * top, most, lean, True), load_shares(amount, rows * top, most, lean, False)
    places = jnp.arange(amount)

    def named(tallies, offset_by):
        used = int((tallies > 0).sum())
        fixed = max(1, used // 4)
        shifted = fixed + (places - fixed + offset_by * (used - fixed)) % max(1, amount - fixed)
        return jnp.zeros((amount,), jnp.int32).at[order[jnp.where(places < fixed, places, shifted)]].set(jnp.asarray(tallies, jnp.int32))

    tallies = jnp.where(number % 4 == 0, named(packed, number // 4), named(ordinary, number - number // 4 - 1))
    mixed = jax.random.permutation(jax.random.fold_in(own, 3), amount)
    donor, sink = mixed[0:amount // 2 * 2:2], mixed[1:amount // 2 * 2:2]
    slack = jnp.minimum(tallies[donor] - 1, most - tallies[sink]) // 2
    slack = jnp.where((donor == order[0]) | (sink == order[0]) | (tallies[sink] == 0), 0, jnp.maximum(slack, 0))
    shifted = jax.random.randint(jax.random.fold_in(own, 4), (amount // 2,), 0, 1 << 20) % (slack + 1)
    tallies = tallies.at[donor].add(-shifted).at[sink].add(shifted)
    members = jnp.searchsorted(jnp.cumsum(tallies), jnp.arange(rows * top), side="right").astype(jnp.int32)
    table = members.reshape(top, rows).T
    table = table[jax.random.permutation(jax.random.fold_in(own, 1), rows)]
    offset_by = jax.random.randint(jax.random.fold_in(own, 2), (rows, 1), 0, top)
    return jnp.take_along_axis(table, (jnp.arange(top)[None, :] + offset_by) % top, axis=1)


def load_shares(amount, total, most, skew, full):
    portions = [(1 << 20) // math.isqrt(standing ** skew) + 1 for standing in range(1, amount + 1)]
    largest = most if full else min(most, max(-(-total // amount), total * portions[0] // sum(portions)))
    least = 1 if total - largest >= amount - 1 else 0
    holding, spare = [largest] + [least] * (amount - 1), total - largest - least * (amount - 1)
    while spare > 0:
        movable = [i for i in range(1, amount) if holding[i] < largest] or [i for i in range(1, amount) if holding[i] < most]
        mass, left = sum([portions[i] for i in movable]), spare
        for i in movable:
            extra = min(most - holding[i], max(1, left * portions[i] // mass), spare)
            holding[i] = holding[i] + extra
            spare = spare - extra
    return np.array(holding)


def noise(key, shape, deviation, bound, split=(), kind=jnp.bfloat16):
    result = deviation * jax.random.normal(key, shape, jnp.float32)
    if split:
        result = result * levels(key, shape, split, -0.22, 0.18)
    return jnp.clip(result, -bound, bound).astype(kind)


def setup_inputs(seed: int = 0) -> dict:
    splits = jax.random.split(jax.random.key(seed), 13)
    act_send = noise(splits[0], (TOKENS, D), 1.0, 6.0, ((0, 32),))
    grad_send = noise(splits[1], (TOKENS, D), 1.0, 6.0, ((0, 32),))
    x_back = noise(splits[2], (TOKENS, D), 1.0, 6.0, ((0, 32),))
    routes_fwd_keys = jax.random.split(jax.random.fold_in(splits[3], 1), TOKENS // TOK_DEV)
    routes_fwd_turns = jax.random.permutation(jax.random.fold_in(splits[3], 3), TOKENS // TOK_DEV)
    routes_fwd = jax.vmap(lambda own, number: assign_block(jax.random.fold_in(splits[3], 2), own, number, TOK_DEV, EXPERTS, TOP, CAP, 2))(routes_fwd_keys, routes_fwd_turns).reshape((TOKENS, TOP))
    gates_fwd = jnp.clip(0.3 + 0.7 * jax.random.uniform(splits[4], (TOKENS, TOP), jnp.float32) ** levels(splits[4], (TOKENS, TOP), ((0, 32),), -0.2, 0.2), 0.3, 1.0)
    routes_back_keys = jax.random.split(jax.random.fold_in(splits[5], 1), TOKENS // TOK_DEV)
    routes_back_turns = jax.random.permutation(jax.random.fold_in(splits[5], 3), TOKENS // TOK_DEV)
    routes_back = jax.vmap(lambda own, number: assign_block(jax.random.fold_in(splits[5], 2), own, number, TOK_DEV, EXPERTS, TOP, CAP, 2))(routes_back_keys, routes_back_turns).reshape((TOKENS, TOP))
    gates_back = jnp.clip(0.3 + 0.7 * jax.random.uniform(splits[6], (TOKENS, TOP), jnp.float32) ** levels(splits[6], (TOKENS, TOP), ((0, 32),), -0.2, 0.2), 0.3, 1.0)
    norm_gain = jnp.clip(1.0 + 0.1 * jax.random.normal(splits[7], (N_SECTION, D), jnp.float32), 0.5, 1.5)
    w_gate = noise(splits[8], (N_SECTION, N_EXPERT, D, HID_DEV), D ** -0.5, 0.09375, ((1, 32),))
    w_up = noise(splits[9], (N_SECTION, N_EXPERT, D, HID_DEV), D ** -0.5, 0.09375, ((1, 32),))
    w_down = noise(splits[10], (N_SECTION, N_EXPERT, HID_DEV, D), EXP_HIDDEN ** -0.5, 0.1875, ((1, 32),))
    stash = noise(splits[11], (N_SECTION, N_EXPERT, N_EXPERT, CAP, 2 * HID_DEV), 1.0, 6.0, ((1, 32),))
    return dict(act_send=act_send, grad_send=grad_send, x_back=x_back, routes_fwd=routes_fwd, gates_fwd=gates_fwd, routes_back=routes_back, gates_back=gates_back, norm_gain=norm_gain, w_gate=w_gate, w_up=w_up, w_down=w_down, stash=stash)


EPSILON = 1e-06
HIGHEST = lax.Precision.HIGHEST

def slot_tables(routes, gates, experts, capacity):
    tokens_here = routes.shape[0]
    chosen = routes.reshape(-1)
    onehot = (chosen[:, None] == jnp.arange(experts, dtype=jnp.int32)[None, :]).astype(jnp.int32)
    earlier = jnp.cumsum(onehot, axis=0) - onehot
    within = lax.optimization_barrier(jnp.sum(earlier * onehot, axis=1))
    target = chosen * capacity + within
    slot_table = (target[:, None] == jnp.arange(experts * capacity, dtype=jnp.int32)[None, :]).astype(jnp.float32)
    slot_table = slot_table.reshape(tokens_here, routes.shape[1], experts * capacity)
    occupancy = lax.optimization_barrier(jnp.sum(slot_table, axis=1)).T
    weighted = lax.optimization_barrier(jnp.sum(slot_table * gates[:, :, None].astype(jnp.float32), axis=1))
    return (occupancy, weighted)

def normalize(values, scale_row):
    factor = lax.rsqrt(lax.optimization_barrier(jnp.mean(values * values, axis=-1, keepdims=True)) + EPSILON)
    return (values * factor * scale_row, factor)

def section_pass(inputs):
    inbound, cotangent, saved_input, routes_fwd, gates_fwd, routes_back, gates_back, scale_row, gate_all, up_all, down_all, stash_all = inputs
    normed = normalize(inbound.astype(jnp.float32), scale_row)[0].astype(jnp.bfloat16)
    tables_fwd = jax.vmap(lambda routes, gates: slot_tables(routes, gates, EXPERTS, CAP))(routes_fwd, gates_fwd)
    occupancy_fwd, weighted_fwd = tables_fwd
    slot_rows = jnp.einsum('skt,std->skd', occupancy_fwd, normed.astype(jnp.float32)).astype(jnp.bfloat16)
    slot_rows = slot_rows.reshape(N_EXPERT, EXPERTS, CAP, D)

    def device_forward(device):
        inputs_here = jnp.take(slot_rows, device // SPLIT, axis=1).reshape(-1, D)
        gate_pre = jnp.dot(inputs_here, gate_all[device], preferred_element_type=jnp.float32)
        up_pre = jnp.dot(inputs_here, up_all[device], preferred_element_type=jnp.float32)
        hidden = (jax.nn.silu(gate_pre) * up_pre).astype(jnp.bfloat16)
        return jnp.dot(hidden, down_all[device], preferred_element_type=jnp.float32).astype(jnp.bfloat16)
    partials = lax.map(device_forward, jnp.arange(N_EXPERT, dtype=jnp.int32))
    summed = partials.astype(jnp.float32).reshape(EXPERTS, SPLIT, N_EXPERT, CAP, D).sum(axis=1)
    summed = summed.transpose(1, 0, 2, 3).reshape(N_EXPERT, EXPERTS * CAP, D)
    mixture = jnp.einsum('stk,skd->std', weighted_fwd, summed, precision=HIGHEST)
    outbound = (inbound.astype(jnp.float32) + mixture).astype(jnp.bfloat16)
    tables_back = jax.vmap(lambda routes, gates: slot_tables(routes, gates, EXPERTS, CAP))(routes_back, gates_back)
    occupancy_back, weighted_back = tables_back
    grad_rows = jnp.einsum('stk,std->skd', weighted_back, cotangent.astype(jnp.float32), precision=HIGHEST).astype(jnp.bfloat16)
    grad_rows = grad_rows.reshape(N_EXPERT, EXPERTS, CAP, D)

    def device_backward(device):
        grad_here = jnp.take(grad_rows, device // SPLIT, axis=1).reshape(-1, D)
        saved_pre = stash_all[device].reshape(-1, 2 * HID_DEV).astype(jnp.float32)
        gate_pre = saved_pre[:, :HID_DEV]
        up_pre = saved_pre[:, HID_DEV:]
        grad_hidden = jnp.dot(grad_here, down_all[device].T, preferred_element_type=jnp.float32)
        sigmoid = jax.nn.sigmoid(gate_pre)
        d_gate = (grad_hidden * up_pre * sigmoid * (1.0 + gate_pre * (1.0 - sigmoid))).astype(jnp.bfloat16)
        d_up = (grad_hidden * gate_pre * sigmoid).astype(jnp.bfloat16)
        total = jnp.dot(d_gate, gate_all[device].T, preferred_element_type=jnp.float32)
        total = total + jnp.dot(d_up, up_all[device].T, preferred_element_type=jnp.float32)
        return total.astype(jnp.bfloat16)
    grad_parts = lax.map(device_backward, jnp.arange(N_EXPERT, dtype=jnp.int32))
    grad_summed = grad_parts.astype(jnp.float32).reshape(EXPERTS, SPLIT, N_EXPERT, CAP, D).sum(axis=1)
    grad_summed = grad_summed.transpose(1, 0, 2, 3).reshape(N_EXPERT, EXPERTS * CAP, D)
    grad_normed = jnp.einsum('skt,skd->std', occupancy_back, grad_summed, precision=HIGHEST)
    saved32 = saved_input.astype(jnp.float32)
    factor = normalize(saved32, scale_row)[1]
    scaled_grad = grad_normed * scale_row
    through = factor * scaled_grad - saved32 * factor ** 3 * lax.optimization_barrier(jnp.mean(scaled_grad * saved32, axis=-1, keepdims=True))
    input_grad = (cotangent.astype(jnp.float32) + through).astype(jnp.bfloat16)
    return (outbound, input_grad)

def reference(act_send, grad_send, x_back, routes_fwd, gates_fwd, routes_back, gates_back, norm_gain, w_gate, w_up, w_down, stash):

    def blocks(array):
        return array.reshape(N_SECTION, N_EXPERT, TOK_DEV, array.shape[-1])
    inbound = jnp.roll(blocks(act_send), 1, axis=0)
    cotangent = jnp.roll(blocks(grad_send), -1, axis=0)
    results = lax.map(section_pass, (inbound, cotangent, blocks(x_back), blocks(routes_fwd), blocks(gates_fwd), blocks(routes_back), blocks(gates_back), norm_gain, w_gate, w_up, w_down, stash))
    outbound, input_grad = results
    return (outbound.reshape(TOKENS, D), input_grad.reshape(TOKENS, D))
```

```python
import jax
import jax.numpy as jnp
from jax import lax
from jax.sharding import PartitionSpec as P

EPSILON = 1e-06
HIGHEST = lax.Precision.HIGHEST
F32 = jnp.float32
BF16 = jnp.bfloat16


def from_behind(value, axis, by):
    size = lax.axis_size(axis)
    if size == 1:
        return value
    return lax.ppermute(value, axis, [(i, (i + by) % size) for i in range(size)])


def swap(value, mask_of):
    size = lax.axis_size("expert")
    return lax.ppermute(value, "expert", [(i, i ^ mask_of(i)) for i in range(size)])


def with_core(value):
    return swap(value, lambda i: 1)


def with_first(value):
    return swap(value, lambda i: 4 if i & 1 else 2)


def with_second(value):
    return swap(value, lambda i: 2 if i & 1 else 4)


def slot_tables(routes, gates, experts, capacity):
    tokens_here = routes.shape[0]
    chosen = routes.reshape(-1)
    onehot = (chosen[:, None] == jnp.arange(experts, dtype=jnp.int32)[None, :]).astype(jnp.int32)
    earlier = jnp.cumsum(onehot, axis=0) - onehot
    within = jnp.sum(earlier * onehot, axis=1)
    target = chosen * capacity + within
    slot_table = (
        target[:, None] == jnp.arange(experts * capacity, dtype=jnp.int32)[None, :]
    ).astype(F32)
    slot_table = slot_table.reshape(tokens_here, routes.shape[1], experts * capacity)
    occupancy = jnp.sum(slot_table, axis=1).T
    weighted = jnp.sum(slot_table * gates[:, :, None], axis=1)
    return (occupancy, weighted)


def normalize(values, scale_row):
    factor = lax.rsqrt(jnp.mean(values * values, axis=-1, keepdims=True) + EPSILON)
    return (values * factor * scale_row, factor)


def dispatch(slot_rows, groups):
    capacity = slot_rows.shape[0] // groups
    chunks = [slot_rows[k * capacity : (k + 1) * capacity] for k in range(groups)]
    arrived = [chunks[0]] + [swap(chunks[k], lambda i, k=k: 8 * k) for k in range(1, groups)]
    own = jnp.concatenate(arrived, axis=0)
    half = jnp.concatenate([own, with_first(own)], axis=0)
    return jnp.concatenate([half, with_second(half)], axis=0)


def give_back(partial_value, groups):
    rows = partial_value.shape[0]
    half, quarter = rows // 2, rows // 4
    arrived = with_second(partial_value[half:].astype(BF16))
    summed = partial_value[:half] + arrived.astype(F32)
    arrived = with_first(summed[quarter:].astype(BF16))
    summed = (summed[:quarter] + arrived.astype(F32)).astype(BF16)
    capacity = quarter // groups
    chunks = [summed[k * capacity : (k + 1) * capacity] for k in range(groups)]
    arrived = [chunks[0]] + [swap(chunks[k], lambda i, k=k: 8 * k) for k in range(1, groups)]
    return jnp.concatenate(arrived, axis=0)


def stash_rows(stash_flat, group, place, core, groups, capacity):
    first = jnp.where(core == 0, 2, 4)
    second = 6 - first
    position = jnp.arange(4 * groups * capacity, dtype=jnp.int32)
    quarter = position // (groups * capacity)
    chunk = position // capacity % groups
    slot = position % capacity
    away = jnp.where(quarter % 2 == 1, first, 0) ^ jnp.where(quarter >= 2, second, 0)
    source = (group ^ chunk) * 8 + ((place & 6) ^ away) + core
    wanted = source * capacity + slot
    table = (
        wanted[:, None] == jnp.arange(stash_flat.shape[0], dtype=jnp.int32)[None, :]
    ).astype(BF16)
    return jnp.dot(table, stash_flat, preferred_element_type=F32).astype(BF16)


def body(
    act_send,
    grad_send,
    x_back,
    routes_fwd,
    gates_fwd,
    routes_back,
    gates_back,
    norm_gain,
    w_gate,
    w_up,
    w_down,
    stash,
):
    sources = lax.axis_size("expert")
    groups = sources // 8
    capacity = stash.shape[3]
    hidden_dev = w_gate.shape[3]
    hidden_two = 2 * hidden_dev
    index = lax.axis_index("expert")
    group, place, core = index // 8, index % 8, index % 2
    scale_row = norm_gain[0]

    gate_other = with_core(w_gate[0, 0])
    up_other = with_core(w_up[0, 0])
    down_other = with_core(w_down[0, 0])
    w_in = jnp.concatenate([w_gate[0, 0], gate_other, w_up[0, 0], up_other], axis=1)
    w_out = jnp.concatenate([w_down[0, 0], down_other], axis=0)

    stash_flat = stash[0, 0].reshape(sources * capacity, 2 * hidden_dev)
    stash_own = stash_rows(stash_flat, group, place, core, groups, capacity)
    stash_other = with_core(stash_rows(stash_flat, group, place, 1 - core, groups, capacity))
    saved_gate = jnp.concatenate(
        [stash_own[:, :hidden_dev], stash_other[:, :hidden_dev]], axis=1
    ).astype(F32)
    saved_up = jnp.concatenate(
        [stash_own[:, hidden_dev:], stash_other[:, hidden_dev:]], axis=1
    ).astype(F32)

    inbound = from_behind(act_send, "section", 1)
    cotangent = from_behind(grad_send, "section", -1)
    occupancy_fwd, weighted_fwd = slot_tables(routes_fwd ^ group, gates_fwd, groups, capacity)
    occupancy_back, weighted_back = slot_tables(routes_back ^ group, gates_back, groups, capacity)

    normed = normalize(inbound.astype(F32), scale_row)[0].astype(BF16)
    slot_rows = jnp.dot(
        occupancy_fwd.astype(BF16), normed, preferred_element_type=F32
    ).astype(BF16)
    flat_rows = dispatch(slot_rows, groups)

    grad_rows = jnp.dot(weighted_back.T, cotangent.astype(F32), precision=HIGHEST).astype(BF16)
    grad_flat = dispatch(grad_rows, groups)

    pre = jnp.dot(flat_rows, w_in, preferred_element_type=F32)
    hidden = (jax.nn.silu(pre[:, :hidden_two]) * pre[:, hidden_two:]).astype(BF16)
    summed = give_back(jnp.dot(hidden, w_out, preferred_element_type=F32), groups)
    mixture = jnp.dot(weighted_fwd, summed.astype(F32), precision=HIGHEST)
    outbound = (inbound.astype(F32) + mixture).astype(BF16)

    grad_hidden = jnp.einsum("rd,hd->rh", grad_flat, w_out, preferred_element_type=F32)
    sigmoid = jax.nn.sigmoid(saved_gate)
    d_gate = (grad_hidden * saved_up * sigmoid * (1.0 + saved_gate * (1.0 - sigmoid))).astype(BF16)
    d_up = (grad_hidden * saved_gate * sigmoid).astype(BF16)
    d_pre = jnp.concatenate([d_gate, d_up], axis=1)
    grad_total = jnp.einsum("rh,dh->rd", d_pre, w_in, preferred_element_type=F32)
    grad_summed = give_back(grad_total, groups)
    grad_normed = jnp.dot(occupancy_back.T, grad_summed.astype(F32), precision=HIGHEST)
    saved32 = x_back.astype(F32)
    factor = normalize(saved32, scale_row)[1]
    scaled_grad = grad_normed * scale_row
    through = factor * scaled_grad - saved32 * factor**3 * jnp.mean(
        scaled_grad * saved32, axis=-1, keepdims=True
    )
    input_grad = (cotangent.astype(F32) + through).astype(BF16)
    return (outbound, input_grad)


def solution(mesh):
    placed = (
        P(("section", "expert"), None),
        P(("section", "expert"), None),
        P(("section", "expert"), None),
        P(("section", "expert"), None),
        P(("section", "expert"), None),
        P(("section", "expert"), None),
        P(("section", "expert"), None),
        P("section", None),
        P("section", "expert", None, None),
        P("section", "expert", None, None),
        P("section", "expert", None, None),
        P("section", "expert", None, None, None),
    )
    return jax.shard_map(
        body,
        mesh=mesh,
        in_specs=placed,
        out_specs=(P(("section", "expert"), None), P(("section", "expert"), None)),
        check_vma=False,
    )
```

```python
import functools

import jax
import jax.numpy as jnp
from jax import lax
from jax.experimental import pallas as pl
from jax.experimental.pallas import tpu as pltpu
from jax.sharding import PartitionSpec as P

EPSILON = 1e-06
HIGHEST = lax.Precision.HIGHEST
F32 = jnp.float32
BF16 = jnp.bfloat16


def from_behind(value, axis, by):
    size = lax.axis_size(axis)
    if size == 1:
        return value
    return lax.ppermute(value, axis, [(i, (i + by) % size) for i in range(size)])


def swap(value, mask_of):
    size = lax.axis_size("expert")
    return lax.ppermute(value, "expert", [(i, i ^ mask_of(i)) for i in range(size)])


def with_core(value):
    return swap(value, lambda i: 1)


def with_first(value):
    return swap(value, lambda i: 4 if i & 1 else 2)


def with_second(value):
    return swap(value, lambda i: 2 if i & 1 else 4)


def slot_table(routes, gates, experts, capacity):
    tokens = routes.shape[1]
    slots = experts * capacity
    slot = lax.broadcasted_iota(jnp.int32, (slots, tokens), 0)
    token = lax.broadcasted_iota(jnp.int32, (slots, tokens), 1)
    expert, place = slot // capacity, slot % capacity
    first = routes[0:1, :] == expert
    second = routes[1:2, :] == expert
    named = jnp.where(first | second, 1.0, 0.0)
    rank = jnp.zeros((slots, tokens), F32)
    for t in range(tokens - 1):
        rank = rank + jnp.where(token > t, named[:, t : t + 1], 0.0)
    here = (named > 0.0) & (rank == place.astype(F32))
    occupied = jnp.where(here, 1.0, 0.0)
    weighted = jnp.where(here, jnp.where(first, gates[0:1, :], gates[1:2, :]), 0.0)
    return occupied, weighted


def prepare_kernel(
    groups,
    capacity,
    inbound_ref,
    cotangent_ref,
    scale_ref,
    routes_fwd_ref,
    gates_fwd_ref,
    routes_back_ref,
    gates_back_ref,
    rows_ref,
    grad_rows_ref,
    weighted_ref,
    occupied_ref,
):
    occupied, weighted = slot_table(routes_fwd_ref[...], gates_fwd_ref[...], groups, capacity)
    inbound = inbound_ref[...].astype(F32)
    factor = lax.rsqrt(jnp.mean(inbound * inbound, axis=-1, keepdims=True) + EPSILON)
    normed = (inbound * factor * scale_ref[...]).astype(BF16)
    rows_ref[...] = jnp.dot(
        occupied.astype(BF16), normed, preferred_element_type=F32
    ).astype(BF16)
    weighted_ref[...] = weighted
    occupied, weighted = slot_table(routes_back_ref[...], gates_back_ref[...], groups, capacity)
    gate = jnp.sum(weighted, axis=1, keepdims=True)
    grad_rows_ref[...] = (
        jnp.dot(occupied.astype(BF16), cotangent_ref[...], preferred_element_type=F32) * gate
    ).astype(BF16)
    occupied_ref[...] = occupied


def prepare(groups, capacity, inbound, cotangent, scale, routes_fwd, gates_fwd, routes_back, gates_back):
    tokens, columns = inbound.shape
    slots = groups * capacity
    return pl.pallas_call(
        functools.partial(prepare_kernel, groups, capacity),
        out_shape=(
            jax.ShapeDtypeStruct((slots, columns), BF16),
            jax.ShapeDtypeStruct((slots, columns), BF16),
            jax.ShapeDtypeStruct((slots, tokens), F32),
            jax.ShapeDtypeStruct((slots, tokens), F32),
        ),
        name="prepare",
    )(inbound, cotangent, scale, routes_fwd, gates_fwd, routes_back, gates_back)


def normalize(values, scale_row):
    factor = lax.rsqrt(jnp.mean(values * values, axis=-1, keepdims=True) + EPSILON)
    return (values * factor * scale_row, factor)


def along_groups(slot_rows, groups):
    capacity = slot_rows.shape[0] // groups
    chunks = [slot_rows[k * capacity : (k + 1) * capacity] for k in range(groups)]
    arrived = [chunks[0]] + [swap(chunks[k], lambda i, k=k: 8 * k) for k in range(1, groups)]
    return jnp.concatenate(arrived, axis=0)


def within_group(own):
    half = jnp.concatenate([own, with_first(own)], axis=0)
    return jnp.concatenate([half, with_second(half)], axis=0)


def give_back(partial_value, groups):
    rows = partial_value.shape[0]
    half, quarter = rows // 2, rows // 4
    arrived = with_second(partial_value[half:].astype(BF16))
    summed = partial_value[:half] + arrived.astype(F32)
    arrived = with_first(summed[quarter:].astype(BF16))
    summed = (summed[:quarter] + arrived.astype(F32)).astype(BF16)
    return along_groups(summed, groups)


def stash_rows(stash_flat, group, place, core, groups, capacity):
    first = jnp.where(core == 0, 2, 4)
    second = 6 - first
    position = jnp.arange(4 * groups * capacity, dtype=jnp.int32)
    quarter = position // (groups * capacity)
    chunk = position // capacity % groups
    slot = position % capacity
    away = jnp.where(quarter % 2 == 1, first, 0) ^ jnp.where(quarter >= 2, second, 0)
    source = (group ^ chunk) * 8 + ((place & 6) ^ away) + core
    wanted = source * capacity + slot
    table = (
        wanted[:, None] == jnp.arange(stash_flat.shape[0], dtype=jnp.int32)[None, :]
    ).astype(BF16)
    return jnp.dot(table, stash_flat, preferred_element_type=F32).astype(BF16)


def body(
    act_send,
    grad_send,
    x_back,
    routes_fwd,
    gates_fwd,
    routes_back,
    gates_back,
    norm_gain,
    w_gate,
    w_up,
    w_down,
    stash,
):
    sources = lax.axis_size("expert")
    groups = sources // 8
    capacity = stash.shape[3]
    hidden_dev = w_gate.shape[3]
    hidden_two = 2 * hidden_dev
    index = lax.axis_index("expert")
    group, place, core = index // 8, index % 8, index % 2
    scale_row = norm_gain[0]

    stash_flat = stash[0, 0].reshape(sources * capacity, 2 * hidden_dev)
    stash_own = stash_rows(stash_flat, group, place, core, groups, capacity)
    stash_other = with_core(stash_rows(stash_flat, group, place, 1 - core, groups, capacity))
    saved_gate = jnp.concatenate(
        [stash_own[:, :hidden_dev], stash_other[:, :hidden_dev]], axis=1
    ).astype(F32)
    saved_up = jnp.concatenate(
        [stash_own[:, hidden_dev:], stash_other[:, hidden_dev:]], axis=1
    ).astype(F32)

    inbound = from_behind(act_send, "section", 1)
    cotangent = from_behind(grad_send, "section", -1)
    slot_rows, grad_rows, weighted_fwd, occupied_back = prepare(
        groups,
        capacity,
        inbound,
        cotangent,
        norm_gain,
        routes_fwd.T ^ group,
        gates_fwd.T,
        routes_back.T ^ group,
        gates_back.T,
    )
    own = along_groups(slot_rows, groups)
    w_gate, w_up, w_down, own = lax.optimization_barrier((w_gate, w_up, w_down, own))
    gate_other = with_core(w_gate[0, 0])
    up_other = with_core(w_up[0, 0])
    down_other = with_core(w_down[0, 0])
    w_in = jnp.concatenate([w_gate[0, 0], gate_other, w_up[0, 0], up_other], axis=1)
    w_out = jnp.concatenate([w_down[0, 0], down_other], axis=0)
    flat_rows = within_group(own)
    grad_own = along_groups(grad_rows, groups)
    grad_flat = within_group(grad_own)

    pre = jnp.dot(flat_rows, w_in, preferred_element_type=F32)
    hidden = (jax.nn.silu(pre[:, :hidden_two]) * pre[:, hidden_two:]).astype(BF16)
    summed = give_back(jnp.dot(hidden, w_out, preferred_element_type=F32), groups)
    mixture = jnp.dot(weighted_fwd.T, summed.astype(F32), precision=HIGHEST)
    outbound = (inbound.astype(F32) + mixture).astype(BF16)

    grad_hidden = jnp.einsum("rd,hd->rh", grad_flat, w_out, preferred_element_type=F32)
    sigmoid = jax.nn.sigmoid(saved_gate)
    d_gate = (grad_hidden * saved_up * sigmoid * (1.0 + saved_gate * (1.0 - sigmoid))).astype(BF16)
    d_up = (grad_hidden * saved_gate * sigmoid).astype(BF16)
    d_pre = jnp.concatenate([d_gate, d_up], axis=1)
    grad_total = jnp.einsum("rh,dh->rd", d_pre, w_in, preferred_element_type=F32)
    grad_summed = give_back(grad_total, groups)
    grad_normed = jnp.dot(occupied_back.T, grad_summed.astype(F32), precision=HIGHEST)
    saved32 = x_back.astype(F32)
    factor = normalize(saved32, scale_row)[1]
    scaled_grad = grad_normed * scale_row
    through = factor * scaled_grad - saved32 * factor**3 * jnp.mean(
        scaled_grad * saved32, axis=-1, keepdims=True
    )
    input_grad = (cotangent.astype(F32) + through).astype(BF16)
    return (outbound, input_grad)


def solution(mesh):
    placed = (
        P(("section", "expert"), None),
        P(("section", "expert"), None),
        P(("section", "expert"), None),
        P(("section", "expert"), None),
        P(("section", "expert"), None),
        P(("section", "expert"), None),
        P(("section", "expert"), None),
        P("section", None),
        P("section", "expert", None, None),
        P("section", "expert", None, None),
        P("section", "expert", None, None),
        P("section", "expert", None, None, None),
    )
    return jax.shard_map(
        body,
        mesh=mesh,
        in_specs=placed,
        out_specs=(P(("section", "expert"), None), P(("section", "expert"), None)),
        check_vma=False,
    )
```

```python
import functools

import jax
import jax.numpy as jnp
from jax import lax
from jax.experimental import pallas as pl
from jax.experimental.pallas import tpu as pltpu
from jax.sharding import PartitionSpec as P

EPSILON = 1e-06
HIGHEST = lax.Precision.HIGHEST
F32 = jnp.float32
BF16 = jnp.bfloat16


def from_behind(value, axis, by):
    size = lax.axis_size(axis)
    if size == 1:
        return value
    return lax.ppermute(value, axis, [(i, (i + by) % size) for i in range(size)])


def swap(value, mask_of):
    size = lax.axis_size("expert")
    return lax.ppermute(value, "expert", [(i, i ^ mask_of(i)) for i in range(size)])


def with_core(value):
    return swap(value, lambda i: 1)


def with_first(value):
    return swap(value, lambda i: 4 if i & 1 else 2)


def with_second(value):
    return swap(value, lambda i: 2 if i & 1 else 4)


def join(parts):
    return jnp.concatenate(parts, axis=0)


def slot_table(routes, gates, experts, capacity):
    tokens = routes.shape[1]
    slots = experts * capacity
    slot = lax.broadcasted_iota(jnp.int32, (slots, tokens), 0)
    token = lax.broadcasted_iota(jnp.int32, (slots, tokens), 1)
    expert, place = slot // capacity, slot % capacity
    first = routes[0:1, :] == expert
    second = routes[1:2, :] == expert
    named = jnp.where(first | second, 1.0, 0.0)
    rank = jnp.zeros((slots, tokens), F32)
    for t in range(tokens - 1):
        rank = rank + jnp.where(token > t, named[:, t : t + 1], 0.0)
    here = (named > 0.0) & (rank == place.astype(F32))
    occupied = jnp.where(here, 1.0, 0.0)
    weighted = jnp.where(here, jnp.where(first, gates[0:1, :], gates[1:2, :]), 0.0)
    return occupied, weighted


def forward_rows_kernel(groups, capacity, inbound_ref, scale_ref, routes_ref, gates_ref, *out_refs):
    group = lax.axis_index("expert") // 8
    occupied, weighted = slot_table(routes_ref[...] ^ group, gates_ref[...], groups, capacity)
    inbound = inbound_ref[...].astype(F32)
    factor = lax.rsqrt(jnp.mean(inbound * inbound, axis=-1, keepdims=True) + EPSILON)
    normed = (inbound * factor * scale_ref[...]).astype(BF16)
    rows = jnp.dot(occupied.astype(BF16), normed, preferred_element_type=F32).astype(BF16)
    for k in range(groups):
        out_refs[k][...] = rows[k * capacity : (k + 1) * capacity]
    out_refs[groups][...] = weighted
    out_refs[groups + 1][...] = jnp.broadcast_to(scale_ref[...], inbound.shape)


def backward_rows_kernel(groups, capacity, cotangent_ref, routes_ref, gates_ref, held_ref, *refs):
    out_refs = refs[:-1]
    refs[-1][...] = held_ref[...]
    group = lax.axis_index("expert") // 8
    occupied, weighted = slot_table(routes_ref[...] ^ group, gates_ref[...], groups, capacity)
    gate = jnp.sum(weighted, axis=1, keepdims=True)
    rows = jnp.dot(occupied.astype(BF16), cotangent_ref[...], preferred_element_type=F32)
    rows = (rows * gate).astype(BF16)
    for k in range(groups):
        out_refs[k][...] = rows[k * capacity : (k + 1) * capacity]
    out_refs[groups][...] = occupied


def in_vmem(value):
    return pltpu.with_memory_space_constraint(value, pltpu.VMEM)


def slot_rows(kernel, name, groups, capacity, value, *rest, held=(), more=()):
    tokens, columns = value.shape
    chunk = pltpu.VMEM((capacity, columns), BF16)
    table = jax.ShapeDtypeStruct((groups * capacity, tokens), F32)
    out = pl.pallas_call(
        functools.partial(kernel, groups, capacity),
        out_shape=(chunk,) * groups + (table,) + (chunk,) * len(held) + more,
        name=name,
        compiler_params=pltpu.CompilerParams(vmem_limit_bytes=4 * 1024 * 1024),
    )(*[pltpu.with_memory_space_constraint(v, pltpu.HBM) for v in (value, *rest)], *[in_vmem(v) for v in held])
    return out[:groups], *out[groups:]


def along_groups(chunks):
    return [chunks[0]] + [swap(chunks[k], lambda i, k=k: 8 * k) for k in range(1, len(chunks))]


def halve(value, exchange):
    rows = value.shape[0] // 2
    return value[:rows] + exchange(value[rows:].astype(BF16)).astype(F32)


def give_back(partial, groups, first, second):
    summed = halve(halve(partial, second), first).astype(BF16)
    capacity = summed.shape[0] // groups
    return join(along_groups([summed[k * capacity : (k + 1) * capacity] for k in range(groups)]))


def stash_rows(stash_flat, group, place, core, groups, capacity):
    first = jnp.where(core == 0, 4, 2)
    second = 6 - first
    position = jnp.arange(4 * groups * capacity, dtype=jnp.int32)
    quarter = position // (groups * capacity)
    chunk = position // capacity % groups
    slot = position % capacity
    away = jnp.where(quarter % 2 == 1, first, 0) ^ jnp.where(quarter >= 2, second, 0)
    source = (group ^ chunk) * 8 + ((place & 6) ^ away) + core
    wanted = source * capacity + slot
    table = (
        wanted[:, None] == jnp.arange(stash_flat.shape[0], dtype=jnp.int32)[None, :]
    ).astype(BF16)
    return jnp.dot(table, stash_flat, preferred_element_type=F32)


def body(
    act_send,
    grad_send,
    x_back,
    routes_fwd,
    gates_fwd,
    routes_back,
    gates_back,
    norm_gain,
    w_gate,
    w_up,
    w_down,
    stash,
):
    sources = lax.axis_size("expert")
    groups = sources // 8
    capacity = stash.shape[3]
    hidden_dev = w_gate.shape[3]
    hidden_two = 2 * hidden_dev
    index = lax.axis_index("expert")
    group, place, core = index // 8, index % 8, index % 2

    inbound = from_behind(act_send, "section", 1)
    cotangent = from_behind(grad_send, "section", -1)
    with jax.named_scope("swaps"):
        gate_other = with_core(w_gate[0, 0])
        up_other = with_core(w_up[0, 0])
        down_other = with_core(w_down[0, 0])
        stash_other = with_core(stash[0, 0])
    chunks, weighted_fwd, scale_rows = slot_rows(
        forward_rows_kernel,
        "forward_rows",
        groups,
        capacity,
        inbound,
        norm_gain,
        routes_fwd.T,
        gates_fwd.T,
        more=(pltpu.VMEM(inbound.shape, F32),),
    )
    with jax.named_scope("forward"):
        arrived = along_groups(chunks)
    routes_back, gate_other, up_other = lax.optimization_barrier(
        (routes_back, gate_other, up_other)
    )
    chunks, occupied_back, own_chunk = slot_rows(
        backward_rows_kernel,
        "backward_rows",
        groups,
        capacity,
        cotangent,
        routes_back.T,
        gates_back.T,
        held=(arrived[0],),
    )
    with jax.named_scope("forward"):
        own = join([own_chunk] + arrived[1:])
    with jax.named_scope("backward"):
        grad_own = join(along_groups(chunks))
    with jax.named_scope("forward"):
        half = join([own, with_first(own)])
        half, stash_other = lax.optimization_barrier(
            (half, stash_other)
        )
        flat_rows = join([half, with_second(half)])
    with jax.named_scope("backward"):
        half = join([grad_own, with_first(grad_own)])
        last = with_second(half)
        rows = grad_own.shape[0]
        grad_flat = join([half[:rows], last[:rows], half[rows:], last[rows:]])

    w_in = jnp.concatenate([w_gate[0, 0], gate_other, w_up[0, 0], up_other], axis=1)
    w_out = join([w_down[0, 0], down_other])
    stash_flat = jnp.concatenate([stash[0, 0], stash_other], axis=2).reshape(sources * capacity, -1)
    saved = stash_rows(stash_flat, group, place, core, groups, capacity)
    saved_gate = jnp.concatenate(
        [saved[:, :hidden_dev], saved[:, hidden_two : hidden_two + hidden_dev]], axis=1
    )
    saved_up = jnp.concatenate(
        [saved[:, hidden_dev:hidden_two], saved[:, hidden_two + hidden_dev :]], axis=1
    )

    pre = jnp.dot(flat_rows, w_in, preferred_element_type=F32)
    hidden = (jax.nn.silu(pre[:, :hidden_two]) * pre[:, hidden_two:]).astype(BF16)
    partial_fwd = jnp.dot(hidden, w_out, preferred_element_type=F32)
    with jax.named_scope("forward"):
        summed = give_back(partial_fwd, groups, with_first, with_second)
    mixture = jnp.dot(weighted_fwd.T, summed.astype(F32), precision=HIGHEST)
    outbound = (inbound.astype(F32) + mixture).astype(BF16)

    grad_hidden = jnp.einsum("rd,hd->rh", grad_flat, w_out, preferred_element_type=F32)
    sigmoid = jax.nn.sigmoid(saved_gate)
    d_gate = (grad_hidden * saved_up * sigmoid * (1.0 + saved_gate * (1.0 - sigmoid))).astype(BF16)
    d_up = (grad_hidden * saved_gate * sigmoid).astype(BF16)
    d_pre = jnp.concatenate([d_gate, d_up], axis=1)
    grad_total = jnp.einsum("rh,dh->rd", d_pre, w_in, preferred_element_type=F32)
    with jax.named_scope("backward"):
        grad_summed = give_back(grad_total, groups, with_second, with_first)
    grad_normed = jnp.dot(occupied_back.T, grad_summed.astype(F32), precision=HIGHEST)
    saved32 = x_back.astype(F32)
    factor = lax.rsqrt(jnp.mean(saved32 * saved32, axis=-1, keepdims=True) + EPSILON)
    scaled_grad = grad_normed * scale_rows
    through = factor * scaled_grad - saved32 * factor**3 * jnp.mean(
        scaled_grad * saved32, axis=-1, keepdims=True
    )
    input_grad = (cotangent.astype(F32) + through).astype(BF16)
    return (outbound, input_grad)


def solution(mesh):
    placed = (
        P(("section", "expert"), None),
        P(("section", "expert"), None),
        P(("section", "expert"), None),
        P(("section", "expert"), None),
        P(("section", "expert"), None),
        P(("section", "expert"), None),
        P(("section", "expert"), None),
        P("section", None),
        P("section", "expert", None, None),
        P("section", "expert", None, None),
        P("section", "expert", None, None),
        P("section", "expert", None, None, None),
    )
    return jax.shard_map(
        body,
        mesh=mesh,
        in_specs=placed,
        out_specs=(P(("section", "expert"), None), P(("section", "expert"), None)),
        check_vma=False,
    )
```

```python
import functools

import jax
import jax.numpy as jnp
from jax import lax
from jax.experimental import pallas as pl
from jax.experimental.pallas import tpu as pltpu
from jax.sharding import PartitionSpec as P

EPSILON = 1e-06
HIGHEST = lax.Precision.HIGHEST
F32 = jnp.float32
BF16 = jnp.bfloat16


def from_behind(value, axis, by):
    size = lax.axis_size(axis)
    if size == 1:
        return value
    return lax.ppermute(value, axis, [(i, (i + by) % size) for i in range(size)])


def swap(value, mask_of):
    size = lax.axis_size("expert")
    return lax.ppermute(value, "expert", [(i, i ^ mask_of(i)) for i in range(size)])


def with_core(value):
    return swap(value, lambda i: 1)


def with_first(value):
    return swap(value, lambda i: 4 if i & 1 else 2)


def with_second(value):
    return swap(value, lambda i: 2 if i & 1 else 4)


def join(parts):
    return jnp.concatenate(parts, axis=0)


def slot_table(routes, gates, experts, capacity):
    tokens = routes.shape[1]
    slots = experts * capacity
    slot = lax.broadcasted_iota(jnp.int32, (slots, tokens), 0)
    token = lax.broadcasted_iota(jnp.int32, (slots, tokens), 1)
    expert, place = slot // capacity, slot % capacity
    first = routes[0:1, :] == expert
    second = routes[1:2, :] == expert
    named = jnp.where(first | second, 1.0, 0.0)
    rank = jnp.zeros((slots, tokens), F32)
    for t in range(tokens - 1):
        rank = rank + jnp.where(token > t, named[:, t : t + 1], 0.0)
    here = (named > 0.0) & (rank == place.astype(F32))
    occupied = jnp.where(here, 1.0, 0.0)
    weighted = jnp.where(here, jnp.where(first, gates[0:1, :], gates[1:2, :]), 0.0)
    return occupied, weighted


def forward_rows_kernel(groups, capacity, inbound_ref, scale_ref, routes_ref, gates_ref, *out_refs):
    group = lax.axis_index("expert") // 8
    occupied, weighted = slot_table(routes_ref[...] ^ group, gates_ref[...], groups, capacity)
    inbound = inbound_ref[...].astype(F32)
    factor = lax.rsqrt(jnp.mean(inbound * inbound, axis=-1, keepdims=True) + EPSILON)
    normed = (inbound * factor * scale_ref[...]).astype(BF16)
    rows = jnp.dot(occupied.astype(BF16), normed, preferred_element_type=F32).astype(BF16)
    for k in range(groups):
        out_refs[k][...] = rows[k * capacity : (k + 1) * capacity]
    out_refs[groups][...] = weighted
    out_refs[groups + 1][...] = jnp.broadcast_to(scale_ref[...], inbound.shape)


def backward_rows_kernel(groups, capacity, cotangent_ref, routes_ref, gates_ref, held_ref, *refs):
    out_refs = refs[:-1]
    refs[-1][...] = held_ref[...]
    group = lax.axis_index("expert") // 8
    occupied, weighted = slot_table(routes_ref[...] ^ group, gates_ref[...], groups, capacity)
    gate = jnp.sum(weighted, axis=1, keepdims=True)
    rows = jnp.dot(occupied.astype(BF16), cotangent_ref[...], preferred_element_type=F32)
    rows = (rows * gate).astype(BF16)
    for k in range(groups):
        out_refs[k][...] = rows[k * capacity : (k + 1) * capacity]
    out_refs[groups][...] = occupied


def in_vmem(value):
    return pltpu.with_memory_space_constraint(value, pltpu.VMEM)


def slot_rows(kernel, name, groups, capacity, value, *rest, held=(), more=()):
    tokens, columns = value.shape
    chunk = pltpu.VMEM((capacity, columns), BF16)
    table = jax.ShapeDtypeStruct((groups * capacity, tokens), F32)
    out = pl.pallas_call(
        functools.partial(kernel, groups, capacity),
        out_shape=(chunk,) * groups + (table,) + (chunk,) * len(held) + more,
        name=name,
        compiler_params=pltpu.CompilerParams(vmem_limit_bytes=4 * 1024 * 1024),
    )(*[pltpu.with_memory_space_constraint(v, pltpu.HBM) for v in (value, *rest)], *[in_vmem(v) for v in held])
    return out[:groups], *out[groups:]


def along_groups(chunks):
    return [chunks[0]] + [swap(chunks[k], lambda i, k=k: 8 * k) for k in range(1, len(chunks))]


def halve(value, exchange):
    rows = value.shape[0] // 2
    return value[:rows] + exchange(value[rows:].astype(BF16)).astype(F32)


def give_back(partial, groups, first, second):
    summed = halve(halve(partial, second), first).astype(BF16)
    capacity = summed.shape[0] // groups
    return join(along_groups([summed[k * capacity : (k + 1) * capacity] for k in range(groups)]))


def stash_rows(stash_flat, group, place, core, groups, capacity):
    first = jnp.where(core == 0, 4, 2)
    second = 6 - first
    position = jnp.arange(4 * groups * capacity, dtype=jnp.int32)
    quarter = position // (groups * capacity)
    chunk = position // capacity % groups
    slot = position % capacity
    away = jnp.where(quarter % 2 == 1, first, 0) ^ jnp.where(quarter >= 2, second, 0)
    source = (group ^ chunk) * 8 + ((place & 6) ^ away) + core
    wanted = source * capacity + slot
    table = (
        wanted[:, None] == jnp.arange(stash_flat.shape[0], dtype=jnp.int32)[None, :]
    ).astype(BF16)
    return jnp.dot(table, stash_flat, preferred_element_type=F32)


def body(
    act_send,
    grad_send,
    x_back,
    routes_fwd,
    gates_fwd,
    routes_back,
    gates_back,
    norm_gain,
    w_gate,
    w_up,
    w_down,
    stash,
):
    sources = lax.axis_size("expert")
    groups = sources // 8
    capacity = stash.shape[3]
    hidden_dev = w_gate.shape[3]
    hidden_two = 2 * hidden_dev
    index = lax.axis_index("expert")
    group, place, core = index // 8, index % 8, index % 2

    inbound = from_behind(act_send, "section", 1)
    cotangent = from_behind(grad_send, "section", -1)
    with jax.named_scope("swaps"):
        gate_other = with_core(w_gate[0, 0])
        up_other = with_core(w_up[0, 0])
        down_other = with_core(w_down[0, 0])
    chunks, weighted_fwd, scale_rows = slot_rows(
        forward_rows_kernel,
        "forward_rows",
        groups,
        capacity,
        inbound,
        norm_gain,
        routes_fwd.T,
        gates_fwd.T,
        more=(pltpu.VMEM(inbound.shape, F32),),
    )
    with jax.named_scope("forward"):
        arrived = along_groups(chunks)
    routes_back, gate_other, up_other = lax.optimization_barrier(
        (routes_back, gate_other, up_other)
    )
    chunks, occupied_back, own_chunk = slot_rows(
        backward_rows_kernel,
        "backward_rows",
        groups,
        capacity,
        cotangent,
        routes_back.T,
        gates_back.T,
        held=(arrived[0],),
    )
    with jax.named_scope("forward"):
        own = join([own_chunk] + arrived[1:])
    with jax.named_scope("backward"):
        grad_own = join(along_groups(chunks))
        grad_own, stash_here = lax.optimization_barrier((grad_own, stash))
        with jax.named_scope("swaps"):
            stash_other = with_core(stash_here[0, 0])
    with jax.named_scope("forward"):
        half = join([own, with_first(own)])
        flat_rows = join([half, with_second(half)])
    with jax.named_scope("backward"):
        half = join([grad_own, with_first(grad_own)])
        last = with_second(half)
        rows = grad_own.shape[0]
        grad_flat = join([half[:rows], last[:rows], half[rows:], last[rows:]])

    w_in = jnp.concatenate([w_gate[0, 0], gate_other, w_up[0, 0], up_other], axis=1)
    w_out = join([w_down[0, 0], down_other])
    stash_flat = jnp.concatenate([stash[0, 0], stash_other], axis=2).reshape(sources * capacity, -1)
    saved = stash_rows(stash_flat, group, place, core, groups, capacity)
    saved_gate = jnp.concatenate(
        [saved[:, :hidden_dev], saved[:, hidden_two : hidden_two + hidden_dev]], axis=1
    )
    saved_up = jnp.concatenate(
        [saved[:, hidden_dev:hidden_two], saved[:, hidden_two + hidden_dev :]], axis=1
    )

    pre = jnp.dot(flat_rows, w_in, preferred_element_type=F32)
    hidden = (jax.nn.silu(pre[:, :hidden_two]) * pre[:, hidden_two:]).astype(BF16)
    partial_fwd = jnp.dot(hidden, w_out, preferred_element_type=F32)
    with jax.named_scope("forward"):
        summed = give_back(partial_fwd, groups, with_first, with_second)
    mixture = jnp.dot(weighted_fwd.T, summed.astype(F32), precision=HIGHEST)
    outbound = (inbound.astype(F32) + mixture).astype(BF16)

    grad_hidden = jnp.einsum("rd,hd->rh", grad_flat, w_out, preferred_element_type=F32)
    sigmoid = jax.nn.sigmoid(saved_gate)
    d_gate = (grad_hidden * saved_up * sigmoid * (1.0 + saved_gate * (1.0 - sigmoid))).astype(BF16)
    d_up = (grad_hidden * saved_gate * sigmoid).astype(BF16)
    d_pre = jnp.concatenate([d_gate, d_up], axis=1)
    grad_total = jnp.einsum("rh,dh->rd", d_pre, w_in, preferred_element_type=F32)
    with jax.named_scope("backward"):
        grad_summed = give_back(grad_total, groups, with_second, with_first)
    grad_normed = jnp.dot(occupied_back.T, grad_summed.astype(F32), precision=HIGHEST)
    saved32 = x_back.astype(F32)
    factor = lax.rsqrt(jnp.mean(saved32 * saved32, axis=-1, keepdims=True) + EPSILON)
    scaled_grad = grad_normed * scale_rows
    through = factor * scaled_grad - saved32 * factor**3 * jnp.mean(
        scaled_grad * saved32, axis=-1, keepdims=True
    )
    input_grad = (cotangent.astype(F32) + through).astype(BF16)
    return (outbound, input_grad)


def solution(mesh):
    placed = (
        P(("section", "expert"), None),
        P(("section", "expert"), None),
        P(("section", "expert"), None),
        P(("section", "expert"), None),
        P(("section", "expert"), None),
        P(("section", "expert"), None),
        P(("section", "expert"), None),
        P("section", None),
        P("section", "expert", None, None),
        P("section", "expert", None, None),
        P("section", "expert", None, None),
        P("section", "expert", None, None, None),
    )
    return jax.shard_map(
        body,
        mesh=mesh,
        in_specs=placed,
        out_specs=(P(("section", "expert"), None), P(("section", "expert"), None)),
        check_vma=False,
    )
```

```python
import functools

import jax
import jax.numpy as jnp
from jax import lax
from jax.experimental import pallas as pl
from jax.experimental.pallas import tpu as pltpu
from jax.sharding import PartitionSpec as P

EPSILON = 1e-06
HIGHEST = lax.Precision.HIGHEST
F32 = jnp.float32
BF16 = jnp.bfloat16


def from_behind(value, axis, by):
    size = lax.axis_size(axis)
    if size == 1:
        return value
    return lax.ppermute(value, axis, [(i, (i + by) % size) for i in range(size)])


def swap(value, mask_of):
    size = lax.axis_size("expert")
    return lax.ppermute(value, "expert", [(i, i ^ mask_of(i)) for i in range(size)])


def with_core(value):
    return swap(value, lambda i: 1)


def with_first(value):
    return swap(value, lambda i: 4 if i & 1 else 2)


def with_second(value):
    return swap(value, lambda i: 2 if i & 1 else 4)


def join(parts):
    return jnp.concatenate(parts, axis=0)


def slot_table(routes, gates, experts, capacity):
    tokens = routes.shape[1]
    slots = experts * capacity
    slot = lax.broadcasted_iota(jnp.int32, (slots, tokens), 0)
    token = lax.broadcasted_iota(jnp.int32, (slots, tokens), 1)
    expert, place = slot // capacity, slot % capacity
    first = routes[0:1, :] == expert
    second = routes[1:2, :] == expert
    named = jnp.where(first | second, 1.0, 0.0)
    rank = jnp.zeros((slots, tokens), F32)
    for t in range(tokens - 1):
        rank = rank + jnp.where(token > t, named[:, t : t + 1], 0.0)
    here = (named > 0.0) & (rank == place.astype(F32))
    occupied = jnp.where(here, 1.0, 0.0)
    weighted = jnp.where(here, jnp.where(first, gates[0:1, :], gates[1:2, :]), 0.0)
    return occupied, weighted


def forward_rows_kernel(groups, capacity, inbound_ref, scale_ref, routes_ref, gates_ref, *out_refs):
    group = lax.axis_index("expert") // 8
    occupied, weighted = slot_table(routes_ref[...] ^ group, gates_ref[...], groups, capacity)
    inbound = inbound_ref[...].astype(F32)
    factor = lax.rsqrt(jnp.mean(inbound * inbound, axis=-1, keepdims=True) + EPSILON)
    normed = (inbound * factor * scale_ref[...]).astype(BF16)
    rows = jnp.dot(occupied.astype(BF16), normed, preferred_element_type=F32).astype(BF16)
    for k in range(groups):
        out_refs[k][...] = rows[k * capacity : (k + 1) * capacity]
    out_refs[groups][...] = weighted
    out_refs[groups + 1][...] = jnp.broadcast_to(scale_ref[...], inbound.shape)


def backward_rows_kernel(groups, capacity, cotangent_ref, routes_ref, gates_ref, held_ref, *refs):
    out_refs = refs[:-1]
    refs[-1][...] = held_ref[...]
    group = lax.axis_index("expert") // 8
    occupied, weighted = slot_table(routes_ref[...] ^ group, gates_ref[...], groups, capacity)
    gate = jnp.sum(weighted, axis=1, keepdims=True)
    rows = jnp.dot(occupied.astype(BF16), cotangent_ref[...], preferred_element_type=F32)
    rows = (rows * gate).astype(BF16)
    for k in range(groups):
        out_refs[k][...] = rows[k * capacity : (k + 1) * capacity]
    out_refs[groups][...] = occupied


def in_vmem(value):
    return pltpu.with_memory_space_constraint(value, pltpu.VMEM)


def slot_rows(kernel, name, groups, capacity, value, *rest, held=(), more=()):
    tokens, columns = value.shape
    chunk = pltpu.VMEM((capacity, columns), BF16)
    table = jax.ShapeDtypeStruct((groups * capacity, tokens), F32)
    out = pl.pallas_call(
        functools.partial(kernel, groups, capacity),
        out_shape=(chunk,) * groups + (table,) + (chunk,) * len(held) + more,
        name=name,
        compiler_params=pltpu.CompilerParams(vmem_limit_bytes=4 * 1024 * 1024),
    )(*[pltpu.with_memory_space_constraint(v, pltpu.HBM) for v in (value, *rest)], *[in_vmem(v) for v in held])
    return out[:groups], *out[groups:]


def along_groups(chunks):
    return [chunks[0]] + [swap(chunks[k], lambda i, k=k: 8 * k) for k in range(1, len(chunks))]


def halve(value, exchange):
    rows = value.shape[0] // 2
    return value[:rows] + exchange(value[rows:].astype(BF16)).astype(F32)


def give_back(partial, groups, first, second):
    summed = halve(halve(partial, second), first).astype(BF16)
    capacity = summed.shape[0] // groups
    return join(along_groups([summed[k * capacity : (k + 1) * capacity] for k in range(groups)]))


def stash_rows(stash_flat, group, place, core, groups, capacity):
    first = jnp.where(core == 0, 4, 2)
    second = 6 - first
    position = jnp.arange(4 * groups * capacity, dtype=jnp.int32)
    quarter = position // (groups * capacity)
    chunk = position // capacity % groups
    slot = position % capacity
    away = jnp.where(quarter % 2 == 1, first, 0) ^ jnp.where(quarter >= 2, second, 0)
    source = (group ^ chunk) * 8 + ((place & 6) ^ away) + core
    wanted = source * capacity + slot
    table = (
        wanted[:, None] == jnp.arange(stash_flat.shape[0], dtype=jnp.int32)[None, :]
    ).astype(BF16)
    return jnp.dot(table, stash_flat, preferred_element_type=F32)


def body(
    act_send,
    grad_send,
    x_back,
    routes_fwd,
    gates_fwd,
    routes_back,
    gates_back,
    norm_gain,
    w_gate,
    w_up,
    w_down,
    stash,
):
    sources = lax.axis_size("expert")
    groups = sources // 8
    capacity = stash.shape[3]
    hidden_dev = w_gate.shape[3]
    hidden_two = 2 * hidden_dev
    index = lax.axis_index("expert")
    group, place, core = index // 8, index % 8, index % 2

    inbound = from_behind(act_send, "section", 1)
    cotangent = from_behind(grad_send, "section", -1)
    with jax.named_scope("swaps"):
        gate_other = with_core(w_gate[0, 0])
        up_other = with_core(w_up[0, 0])
        down_other = with_core(w_down[0, 0])
    chunks, weighted_fwd, scale_rows = slot_rows(
        forward_rows_kernel,
        "forward_rows",
        groups,
        capacity,
        inbound,
        norm_gain,
        routes_fwd.T,
        gates_fwd.T,
        more=(pltpu.VMEM(inbound.shape, F32),),
    )
    with jax.named_scope("forward"):
        arrived = along_groups(chunks)
    routes_back, gate_other, up_other, down_other = lax.optimization_barrier(
        (routes_back, gate_other, up_other, down_other)
    )
    chunks, occupied_back, own_chunk = slot_rows(
        backward_rows_kernel,
        "backward_rows",
        groups,
        capacity,
        cotangent,
        routes_back.T,
        gates_back.T,
        held=(arrived[0],),
    )
    with jax.named_scope("forward"):
        own = join([own_chunk] + arrived[1:])
    with jax.named_scope("backward"):
        grad_own = join(along_groups(chunks))
        grad_own, stash_here = lax.optimization_barrier((grad_own, stash))
        with jax.named_scope("swaps"):
            stash_other = with_core(stash_here[0, 0])
    with jax.named_scope("forward"):
        half = join([own, with_first(own)])
        flat_rows = join([half, with_second(half)])
    with jax.named_scope("backward"):
        half = join([grad_own, with_first(grad_own)])
        last = with_second(half)
        rows = grad_own.shape[0]
        grad_flat = join([half[:rows], last[:rows], half[rows:], last[rows:]])

    w_in = jnp.concatenate([w_gate[0, 0], gate_other, w_up[0, 0], up_other], axis=1)
    w_out = join([w_down[0, 0], down_other])
    stash_flat = jnp.concatenate([stash[0, 0], stash_other], axis=2).reshape(sources * capacity, -1)
    saved = stash_rows(stash_flat, group, place, core, groups, capacity)
    saved_gate = jnp.concatenate(
        [saved[:, :hidden_dev], saved[:, hidden_two : hidden_two + hidden_dev]], axis=1
    )
    saved_up = jnp.concatenate(
        [saved[:, hidden_dev:hidden_two], saved[:, hidden_two + hidden_dev :]], axis=1
    )

    pre = jnp.dot(flat_rows, w_in, preferred_element_type=F32)
    hidden = (jax.nn.silu(pre[:, :hidden_two]) * pre[:, hidden_two:]).astype(BF16)
    partial_fwd = jnp.dot(hidden, w_out, preferred_element_type=F32)
    with jax.named_scope("forward"):
        summed = give_back(partial_fwd, groups, with_first, with_second)
    mixture = jnp.dot(weighted_fwd.T, summed.astype(F32), precision=HIGHEST)
    outbound = (inbound.astype(F32) + mixture).astype(BF16)

    grad_hidden = jnp.einsum("rd,hd->rh", grad_flat, w_out, preferred_element_type=F32)
    sigmoid = jax.nn.sigmoid(saved_gate)
    d_gate = (grad_hidden * saved_up * sigmoid * (1.0 + saved_gate * (1.0 - sigmoid))).astype(BF16)
    d_up = (grad_hidden * saved_gate * sigmoid).astype(BF16)
    d_pre = jnp.concatenate([d_gate, d_up], axis=1)
    grad_total = jnp.einsum("rh,dh->rd", d_pre, w_in, preferred_element_type=F32)
    with jax.named_scope("backward"):
        grad_summed = give_back(grad_total, groups, with_second, with_first)
    grad_normed = jnp.dot(occupied_back.T, grad_summed.astype(F32), precision=HIGHEST)
    saved32 = x_back.astype(F32)
    factor = lax.rsqrt(jnp.mean(saved32 * saved32, axis=-1, keepdims=True) + EPSILON)
    scaled_grad = grad_normed * scale_rows
    through = factor * scaled_grad - saved32 * factor**3 * jnp.mean(
        scaled_grad * saved32, axis=-1, keepdims=True
    )
    input_grad = (cotangent.astype(F32) + through).astype(BF16)
    return (outbound, input_grad)


def solution(mesh):
    placed = (
        P(("section", "expert"), None),
        P(("section", "expert"), None),
        P(("section", "expert"), None),
        P(("section", "expert"), None),
        P(("section", "expert"), None),
        P(("section", "expert"), None),
        P(("section", "expert"), None),
        P("section", None),
        P("section", "expert", None, None),
        P("section", "expert", None, None),
        P("section", "expert", None, None),
        P("section", "expert", None, None, None),
    )
    return jax.shard_map(
        body,
        mesh=mesh,
        in_specs=placed,
        out_specs=(P(("section", "expert"), None), P(("section", "expert"), None)),
        check_vma=False,
    )
```

```python
import functools

import jax
import jax.numpy as jnp
from jax import lax
from jax.experimental import pallas as pl
from jax.experimental.pallas import tpu as pltpu
from jax.sharding import PartitionSpec as P

EPSILON = 1e-06
HIGHEST = lax.Precision.HIGHEST
F32 = jnp.float32
BF16 = jnp.bfloat16


def from_behind(value, axis, by):
    size = lax.axis_size(axis)
    if size == 1:
        return value
    return lax.ppermute(value, axis, [(i, (i + by) % size) for i in range(size)])


def swap(value, mask_of):
    size = lax.axis_size("expert")
    return lax.ppermute(value, "expert", [(i, i ^ mask_of(i)) for i in range(size)])


def with_core(value):
    return swap(value, lambda i: 1)


def with_first(value):
    return swap(value, lambda i: 4 if i & 1 else 2)


def with_second(value):
    return swap(value, lambda i: 2 if i & 1 else 4)


def join(parts):
    return jnp.concatenate(parts, axis=0)


def slot_table(routes, gates, experts, capacity):
    tokens = routes.shape[1]
    slots = experts * capacity
    slot = lax.broadcasted_iota(jnp.int32, (slots, tokens), 0)
    token = lax.broadcasted_iota(jnp.int32, (slots, tokens), 1)
    expert, place = slot // capacity, slot % capacity
    first = routes[0:1, :] == expert
    second = routes[1:2, :] == expert
    named = jnp.where(first | second, 1.0, 0.0)
    rank = jnp.zeros((slots, tokens), F32)
    for t in range(tokens - 1):
        rank = rank + jnp.where(token > t, named[:, t : t + 1], 0.0)
    here = (named > 0.0) & (rank == place.astype(F32))
    occupied = jnp.where(here, 1.0, 0.0)
    weighted = jnp.where(here, jnp.where(first, gates[0:1, :], gates[1:2, :]), 0.0)
    return occupied, weighted


def forward_rows_kernel(groups, capacity, inbound_ref, scale_ref, routes_ref, gates_ref, *out_refs):
    group = lax.axis_index("expert") // 8
    occupied, weighted = slot_table(routes_ref[...] ^ group, gates_ref[...], groups, capacity)
    inbound = inbound_ref[...].astype(F32)
    factor = lax.rsqrt(jnp.mean(inbound * inbound, axis=-1, keepdims=True) + EPSILON)
    normed = (inbound * factor * scale_ref[...]).astype(BF16)
    rows = jnp.dot(occupied.astype(BF16), normed, preferred_element_type=F32).astype(BF16)
    for k in range(groups):
        out_refs[k][...] = rows[k * capacity : (k + 1) * capacity]
    out_refs[groups][...] = weighted
    out_refs[groups + 1][...] = jnp.broadcast_to(scale_ref[...], inbound.shape)


def backward_rows_kernel(groups, capacity, cotangent_ref, routes_ref, gates_ref, held_ref, *refs):
    out_refs = refs[:-1]
    refs[-1][...] = held_ref[...]
    group = lax.axis_index("expert") // 8
    occupied, weighted = slot_table(routes_ref[...] ^ group, gates_ref[...], groups, capacity)
    gate = jnp.sum(weighted, axis=1, keepdims=True)
    rows = jnp.dot(occupied.astype(BF16), cotangent_ref[...], preferred_element_type=F32)
    rows = (rows * gate).astype(BF16)
    for k in range(groups):
        out_refs[k][...] = rows[k * capacity : (k + 1) * capacity]
    out_refs[groups][...] = occupied


def in_vmem(value):
    return pltpu.with_memory_space_constraint(value, pltpu.VMEM)


def slot_rows(kernel, name, groups, capacity, value, *rest, held=(), more=()):
    tokens, columns = value.shape
    chunk = pltpu.VMEM((capacity, columns), BF16)
    table = jax.ShapeDtypeStruct((groups * capacity, tokens), F32)
    out = pl.pallas_call(
        functools.partial(kernel, groups, capacity),
        out_shape=(chunk,) * groups + (table,) + (chunk,) * len(held) + more,
        name=name,
        compiler_params=pltpu.CompilerParams(vmem_limit_bytes=4 * 1024 * 1024),
    )(*[pltpu.with_memory_space_constraint(v, pltpu.HBM) for v in (value, *rest)], *[in_vmem(v) for v in held])
    return out[:groups], *out[groups:]


def along_groups(chunks):
    return [chunks[0]] + [swap(chunks[k], lambda i, k=k: 8 * k) for k in range(1, len(chunks))]


def halve(value, exchange):
    rows = value.shape[0] // 2
    return value[:rows] + exchange(value[rows:].astype(BF16)).astype(F32)


def give_back_three(partial, groups, first, second):
    rows = partial.shape[0] // 4
    own, near, side, cross = [partial[q * rows : (q + 1) * rows] for q in range(4)]
    cross = second(cross.astype(BF16)).astype(F32)
    side = second(side.astype(BF16)).astype(F32)
    near = first((near + cross).astype(BF16)).astype(F32)
    summed = (own + side + near).astype(BF16)
    capacity = rows // groups
    return join(along_groups([summed[k * capacity : (k + 1) * capacity] for k in range(groups)]))


def stash_rows(stash_flat, group, place, core, groups, capacity):
    first = jnp.where(core == 0, 4, 2)
    second = 6 - first
    position = jnp.arange(4 * groups * capacity, dtype=jnp.int32)
    quarter = position // (groups * capacity)
    chunk = position // capacity % groups
    slot = position % capacity
    away = jnp.where(quarter % 2 == 1, first, 0) ^ jnp.where(quarter >= 2, second, 0)
    source = (group ^ chunk) * 8 + ((place & 6) ^ away) + core
    wanted = source * capacity + slot
    table = (
        wanted[:, None] == jnp.arange(stash_flat.shape[0], dtype=jnp.int32)[None, :]
    ).astype(BF16)
    return jnp.dot(table, stash_flat, preferred_element_type=F32)


def body(
    act_send,
    grad_send,
    x_back,
    routes_fwd,
    gates_fwd,
    routes_back,
    gates_back,
    norm_gain,
    w_gate,
    w_up,
    w_down,
    stash,
):
    sources = lax.axis_size("expert")
    groups = sources // 8
    capacity = stash.shape[3]
    hidden_dev = w_gate.shape[3]
    hidden_two = 2 * hidden_dev
    index = lax.axis_index("expert")
    group, place, core = index // 8, index % 8, index % 2

    inbound = from_behind(act_send, "section", 1)
    cotangent = from_behind(grad_send, "section", -1)
    with jax.named_scope("swaps"):
        gate_other = with_core(w_gate[0, 0])
        up_other = with_core(w_up[0, 0])
        down_other = with_core(w_down[0, 0])
    chunks, weighted_fwd, scale_rows = slot_rows(
        forward_rows_kernel,
        "forward_rows",
        groups,
        capacity,
        inbound,
        norm_gain,
        routes_fwd.T,
        gates_fwd.T,
        more=(pltpu.VMEM(inbound.shape, F32),),
    )
    with jax.named_scope("forward"):
        arrived = along_groups(chunks)
    routes_back, gate_other, up_other, down_other = lax.optimization_barrier(
        (routes_back, gate_other, up_other, down_other)
    )
    chunks, occupied_back, own_chunk = slot_rows(
        backward_rows_kernel,
        "backward_rows",
        groups,
        capacity,
        cotangent,
        routes_back.T,
        gates_back.T,
        held=(arrived[0],),
    )
    with jax.named_scope("forward"):
        own = join([own_chunk] + arrived[1:])
    with jax.named_scope("backward"):
        grad_own = join(along_groups(chunks))
        grad_own, stash_here = lax.optimization_barrier((grad_own, stash))
        with jax.named_scope("swaps"):
            stash_other = with_core(stash_here[0, 0])
    with jax.named_scope("forward"):
        half = join([own, with_first(own)])
        flat_rows = join([half, with_second(half)])
    with jax.named_scope("backward"):
        half = join([grad_own, with_first(grad_own)])
        last = with_second(half)
        rows = grad_own.shape[0]
        grad_flat = join([half[:rows], last[:rows], half[rows:], last[rows:]])

    w_in = jnp.concatenate([w_gate[0, 0], gate_other, w_up[0, 0], up_other], axis=1)
    w_out = join([w_down[0, 0], down_other])
    stash_flat = jnp.concatenate([stash[0, 0], stash_other], axis=2).reshape(sources * capacity, -1)
    saved = stash_rows(stash_flat, group, place, core, groups, capacity)
    saved_gate = jnp.concatenate(
        [saved[:, :hidden_dev], saved[:, hidden_two : hidden_two + hidden_dev]], axis=1
    )
    saved_up = jnp.concatenate(
        [saved[:, hidden_dev:hidden_two], saved[:, hidden_two + hidden_dev :]], axis=1
    )

    pre = jnp.dot(flat_rows, w_in, preferred_element_type=F32)
    hidden = (jax.nn.silu(pre[:, :hidden_two]) * pre[:, hidden_two:]).astype(BF16)
    partial_fwd = jnp.dot(hidden, w_out, preferred_element_type=F32)
    with jax.named_scope("forward"):
        summed = give_back_three(partial_fwd, groups, with_first, with_second)
    mixture = jnp.dot(weighted_fwd.T, summed.astype(F32), precision=HIGHEST)
    outbound = (inbound.astype(F32) + mixture).astype(BF16)

    grad_hidden = jnp.einsum("rd,hd->rh", grad_flat, w_out, preferred_element_type=F32)
    sigmoid = jax.nn.sigmoid(saved_gate)
    d_gate = (grad_hidden * saved_up * sigmoid * (1.0 + saved_gate * (1.0 - sigmoid))).astype(BF16)
    d_up = (grad_hidden * saved_gate * sigmoid).astype(BF16)
    d_pre = jnp.concatenate([d_gate, d_up], axis=1)
    grad_total = jnp.einsum("rh,dh->rd", d_pre, w_in, preferred_element_type=F32)
    with jax.named_scope("backward"):
        grad_summed = give_back_three(grad_total, groups, with_second, with_first)
    grad_normed = jnp.dot(occupied_back.T, grad_summed.astype(F32), precision=HIGHEST)
    saved32 = x_back.astype(F32)
    factor = lax.rsqrt(jnp.mean(saved32 * saved32, axis=-1, keepdims=True) + EPSILON)
    scaled_grad = grad_normed * scale_rows
    through = factor * scaled_grad - saved32 * factor**3 * jnp.mean(
        scaled_grad * saved32, axis=-1, keepdims=True
    )
    input_grad = (cotangent.astype(F32) + through).astype(BF16)
    return (outbound, input_grad)


def solution(mesh):
    placed = (
        P(("section", "expert"), None),
        P(("section", "expert"), None),
        P(("section", "expert"), None),
        P(("section", "expert"), None),
        P(("section", "expert"), None),
        P(("section", "expert"), None),
        P(("section", "expert"), None),
        P("section", None),
        P("section", "expert", None, None),
        P("section", "expert", None, None),
        P("section", "expert", None, None),
        P("section", "expert", None, None, None),
    )
    return jax.shard_map(
        body,
        mesh=mesh,
        in_specs=placed,
        out_specs=(P(("section", "expert"), None), P(("section", "expert"), None)),
        check_vma=False,
    )
```

```python
import functools

import jax
import jax.numpy as jnp
from jax import lax
from jax.experimental import pallas as pl
from jax.experimental.pallas import tpu as pltpu
from jax.sharding import PartitionSpec as P

EPSILON = 1e-06
HIGHEST = lax.Precision.HIGHEST
F32 = jnp.float32
BF16 = jnp.bfloat16


def from_behind(value, axis, by):
    size = lax.axis_size(axis)
    if size == 1:
        return value
    return lax.ppermute(value, axis, [(i, (i + by) % size) for i in range(size)])


def swap(value, mask_of):
    size = lax.axis_size("expert")
    return lax.ppermute(value, "expert", [(i, i ^ mask_of(i)) for i in range(size)])


def with_core(value):
    return swap(value, lambda i: 1)


def with_first(value):
    return swap(value, lambda i: 4 if i & 1 else 2)


def with_second(value):
    return swap(value, lambda i: 2 if i & 1 else 4)


def join(parts):
    return jnp.concatenate(parts, axis=0)


def slot_table(routes, gates, experts, capacity):
    tokens = routes.shape[1]
    slots = experts * capacity
    slot = lax.broadcasted_iota(jnp.int32, (slots, tokens), 0)
    token = lax.broadcasted_iota(jnp.int32, (slots, tokens), 1)
    expert, place = slot // capacity, slot % capacity
    first = routes[0:1, :] == expert
    second = routes[1:2, :] == expert
    named = jnp.where(first | second, 1.0, 0.0)
    rank = jnp.zeros((slots, tokens), F32)
    for t in range(tokens - 1):
        rank = rank + jnp.where(token > t, named[:, t : t + 1], 0.0)
    here = (named > 0.0) & (rank == place.astype(F32))
    occupied = jnp.where(here, 1.0, 0.0)
    weighted = jnp.where(here, jnp.where(first, gates[0:1, :], gates[1:2, :]), 0.0)
    return occupied, weighted


def forward_rows_kernel(groups, capacity, inbound_ref, scale_ref, routes_ref, gates_ref, *out_refs):
    group = lax.axis_index("expert") // 8
    occupied, weighted = slot_table(routes_ref[...] ^ group, gates_ref[...], groups, capacity)
    inbound = inbound_ref[...].astype(F32)
    factor = lax.rsqrt(jnp.mean(inbound * inbound, axis=-1, keepdims=True) + EPSILON)
    normed = (inbound * factor * scale_ref[...]).astype(BF16)
    rows = jnp.dot(occupied.astype(BF16), normed, preferred_element_type=F32).astype(BF16)
    for k in range(groups):
        out_refs[k][...] = rows[k * capacity : (k + 1) * capacity]
    out_refs[groups][...] = weighted
    out_refs[groups + 1][...] = jnp.broadcast_to(scale_ref[...], inbound.shape)


def backward_rows_kernel(groups, capacity, cotangent_ref, routes_ref, gates_ref, held_ref, *refs):
    out_refs = refs[:-1]
    refs[-1][...] = held_ref[...]
    group = lax.axis_index("expert") // 8
    occupied, weighted = slot_table(routes_ref[...] ^ group, gates_ref[...], groups, capacity)
    gate = jnp.sum(weighted, axis=1, keepdims=True)
    rows = jnp.dot(occupied.astype(BF16), cotangent_ref[...], preferred_element_type=F32)
    rows = (rows * gate).astype(BF16)
    for k in range(groups):
        out_refs[k][...] = rows[k * capacity : (k + 1) * capacity]
    out_refs[groups][...] = occupied


def in_vmem(value):
    return pltpu.with_memory_space_constraint(value, pltpu.VMEM)


def slot_rows(kernel, name, groups, capacity, value, *rest, held=(), more=()):
    tokens, columns = value.shape
    chunk = pltpu.VMEM((capacity, columns), BF16)
    table = jax.ShapeDtypeStruct((groups * capacity, tokens), F32)
    out = pl.pallas_call(
        functools.partial(kernel, groups, capacity),
        out_shape=(chunk,) * groups + (table,) + (chunk,) * len(held) + more,
        name=name,
        compiler_params=pltpu.CompilerParams(vmem_limit_bytes=4 * 1024 * 1024),
    )(*[pltpu.with_memory_space_constraint(v, pltpu.HBM) for v in (value, *rest)], *[in_vmem(v) for v in held])
    return out[:groups], *out[groups:]


def along_groups(chunks):
    arrived = [swap(chunks[k], lambda i, k=k: 8 * k) for k in range(len(chunks) - 1, 0, -1)]
    return [chunks[0]] + arrived[::-1]


def halve(value, exchange):
    rows = value.shape[0] // 2
    return value[:rows] + exchange(value[rows:].astype(BF16)).astype(F32)


def give_back_three(partial, groups, first, second):
    rows = partial.shape[0] // 4
    own, near, side, cross = [partial[q * rows : (q + 1) * rows] for q in range(4)]
    cross = second(cross.astype(BF16)).astype(F32)
    side = second(side.astype(BF16)).astype(F32)
    near = first((near + cross).astype(BF16)).astype(F32)
    summed = (own + side + near).astype(BF16)
    capacity = rows // groups
    return join(along_groups([summed[k * capacity : (k + 1) * capacity] for k in range(groups)]))


def stash_rows(stash_flat, group, place, core, groups, capacity):
    first = jnp.where(core == 0, 4, 2)
    second = 6 - first
    position = jnp.arange(4 * groups * capacity, dtype=jnp.int32)
    quarter = position // (groups * capacity)
    chunk = position // capacity % groups
    slot = position % capacity
    away = jnp.where(quarter % 2 == 1, first, 0) ^ jnp.where(quarter >= 2, second, 0)
    source = (group ^ chunk) * 8 + ((place & 6) ^ away) + core
    wanted = source * capacity + slot
    table = (
        wanted[:, None] == jnp.arange(stash_flat.shape[0], dtype=jnp.int32)[None, :]
    ).astype(BF16)
    return jnp.dot(table, stash_flat, preferred_element_type=F32)


def body(
    act_send,
    grad_send,
    x_back,
    routes_fwd,
    gates_fwd,
    routes_back,
    gates_back,
    norm_gain,
    w_gate,
    w_up,
    w_down,
    stash,
):
    sources = lax.axis_size("expert")
    groups = sources // 8
    capacity = stash.shape[3]
    hidden_dev = w_gate.shape[3]
    hidden_two = 2 * hidden_dev
    index = lax.axis_index("expert")
    group, place, core = index // 8, index % 8, index % 2

    inbound = from_behind(act_send, "section", 1)
    cotangent = from_behind(grad_send, "section", -1)
    with jax.named_scope("swaps"):
        gate_other = with_core(w_gate[0, 0])
        up_other = with_core(w_up[0, 0])
        down_other = with_core(w_down[0, 0])
    chunks, weighted_fwd, scale_rows = slot_rows(
        forward_rows_kernel,
        "forward_rows",
        groups,
        capacity,
        inbound,
        norm_gain,
        routes_fwd.T,
        gates_fwd.T,
        more=(pltpu.VMEM(inbound.shape, F32),),
    )
    with jax.named_scope("forward"):
        arrived = along_groups(chunks)
    routes_back, gate_other, up_other, down_other = lax.optimization_barrier(
        (routes_back, gate_other, up_other, down_other)
    )
    chunks, occupied_back, own_chunk = slot_rows(
        backward_rows_kernel,
        "backward_rows",
        groups,
        capacity,
        cotangent,
        routes_back.T,
        gates_back.T,
        held=(arrived[0],),
    )
    with jax.named_scope("forward"):
        own = join([own_chunk] + arrived[1:])
    with jax.named_scope("backward"):
        grad_own = join(along_groups(chunks))
        grad_own, stash_here = lax.optimization_barrier((grad_own, stash))
        with jax.named_scope("swaps"):
            stash_other = with_core(stash_here[0, 0])
    with jax.named_scope("forward"):
        half = join([own, with_first(own)])
        flat_rows = join([half, with_second(half)])
    with jax.named_scope("backward"):
        half = join([grad_own, with_first(grad_own)])
        last = with_second(half)
        rows = grad_own.shape[0]
        grad_flat = join([half[:rows], last[:rows], half[rows:], last[rows:]])

    w_in = jnp.concatenate([w_gate[0, 0], gate_other, w_up[0, 0], up_other], axis=1)
    w_out = join([w_down[0, 0], down_other])
    stash_flat = jnp.concatenate([stash[0, 0], stash_other], axis=2).reshape(sources * capacity, -1)
    saved = stash_rows(stash_flat, group, place, core, groups, capacity)
    saved_gate = jnp.concatenate(
        [saved[:, :hidden_dev], saved[:, hidden_two : hidden_two + hidden_dev]], axis=1
    )
    saved_up = jnp.concatenate(
        [saved[:, hidden_dev:hidden_two], saved[:, hidden_two + hidden_dev :]], axis=1
    )

    pre = jnp.dot(flat_rows, w_in, preferred_element_type=F32)
    hidden = (jax.nn.silu(pre[:, :hidden_two]) * pre[:, hidden_two:]).astype(BF16)
    partial_fwd = jnp.dot(hidden, w_out, preferred_element_type=F32)
    with jax.named_scope("forward"):
        summed = give_back_three(partial_fwd, groups, with_first, with_second)
    mixture = jnp.dot(weighted_fwd.T, summed.astype(F32), precision=HIGHEST)
    outbound = (inbound.astype(F32) + mixture).astype(BF16)

    grad_hidden = jnp.einsum("rd,hd->rh", grad_flat, w_out, preferred_element_type=F32)
    sigmoid = jax.nn.sigmoid(saved_gate)
    d_gate = (grad_hidden * saved_up * sigmoid * (1.0 + saved_gate * (1.0 - sigmoid))).astype(BF16)
    d_up = (grad_hidden * saved_gate * sigmoid).astype(BF16)
    d_pre = jnp.concatenate([d_gate, d_up], axis=1)
    grad_total = jnp.einsum("rh,dh->rd", d_pre, w_in, preferred_element_type=F32)
    with jax.named_scope("backward"):
        grad_summed = give_back_three(grad_total, groups, with_second, with_first)
    grad_normed = jnp.dot(occupied_back.T, grad_summed.astype(F32), precision=HIGHEST)
    saved32 = x_back.astype(F32)
    factor = lax.rsqrt(jnp.mean(saved32 * saved32, axis=-1, keepdims=True) + EPSILON)
    scaled_grad = grad_normed * scale_rows
    through = factor * scaled_grad - saved32 * factor**3 * jnp.mean(
        scaled_grad * saved32, axis=-1, keepdims=True
    )
    input_grad = (cotangent.astype(F32) + through).astype(BF16)
    return (outbound, input_grad)


def solution(mesh):
    placed = (
        P(("section", "expert"), None),
        P(("section", "expert"), None),
        P(("section", "expert"), None),
        P(("section", "expert"), None),
        P(("section", "expert"), None),
        P(("section", "expert"), None),
        P(("section", "expert"), None),
        P("section", None),
        P("section", "expert", None, None),
        P("section", "expert", None, None),
        P("section", "expert", None, None),
        P("section", "expert", None, None, None),
    )
    return jax.shard_map(
        body,
        mesh=mesh,
        in_specs=placed,
        out_specs=(P(("section", "expert"), None), P(("section", "expert"), None)),
        check_vma=False,
    )
```
